32 devices in a mesh: grp: 4 (over y, core), shard: 8 (over z, x).
Axes of the slice: x: 2, y: 2, z: 4, core: 2. Of those that a mesh axis runs over, the one named last changes fastest.
Arguments:
- table: float32 [32768, 256], P('shard'), may hold values from -6 to 6
- accum: float32 [32768], P('shard'), may hold values from 0.05 to 2
- pooled_grad: bfloat16 [4, 8, 512, 256], P('grp', 'shard'), may hold values from -6 to 6
- row_ids: int32 [4, 8, 4096], P('grp', 'shard'), may hold values from 0 to 32767, as said below
- bag_ids: int32 [4, 8, 4096], P('grp', 'shard'), may hold values from 0 to 511, never falling along the last dimension, each value on 1 to 16 neighbouring positions
- touched: int32 [8, 1024], P('shard'), may hold values from 0 to 4095, as said below
Outputs:
- new_table: float32 [32768, 256], P('shard')
- new_accum: float32 [32768], P('shard')
The draws below stay inside these ranges and needn't reach their ends.
Inputs may be any that keep to these rules, and one draw needn't show every extreme that they name: `row_ids`: every id is s * 4096 + touched[s, k] for some shard s and some k: it lies in a listed row. At most 512 lookups of one device fall on one shard s (ids in s * 4096 to (s + 1) * 4096 - 1); in every draw some device sends exactly 512 to some shard, and in each replica one shard receives 512 from every device of that replica. Each row of touched holds 1024 distinct row numbers in increasing order.
All inputs are finite; a program needn't handle non-finite values.
Results may differ from the reference program's by a relative error of at most 0.0003.
Values may be sent and summed in bfloat16 or wider, within the bound.
A program may use at most 128 MiB of HBM per device.

```python
import math
import jax
import jax.numpy as jnp
import numpy as np
from jax import lax

E = 256
ROWS_DEV = 4096
TOUCH = 1024
LOOK_DEV = 4096
POOL = 8
B_DEV = 512
CAP = 512
ROWS = 32768
N_GRP = 4
N_SHARD = 8


def listed_table(key):
    keys = jax.random.split(jax.random.fold_in(key, 11), N_SHARD)

    def one_shard(shard_key):
        return jnp.sort(jax.random.permutation(shard_key, ROWS_DEV)[:TOUCH]).astype(jnp.int32)
    return jax.vmap(one_shard)(keys)


def draw_touched(key, part):
    return listed_table(key)


def draw_row_ids(key, part):
    listed = listed_table(key)
    base_key = jax.random.fold_in(key, 23)
    hot = jax.random.randint(jax.random.fold_in(base_key, 1), (N_GRP,), 0, N_SHARD)
    offsets = jax.random.randint(jax.random.fold_in(base_key, 2), (N_GRP, N_SHARD), 0, N_SHARD - 1)
    position = jnp.arange(LOOK_DEV - CAP, dtype=jnp.int32)
    hot_full = hot[:, None, None]
    others = (hot_full + 1 + (position[None, None, :] + offsets[:, :, None]) % (N_SHARD - 1)) % N_SHARD
    hot_part = jnp.broadcast_to(hot_full, (N_GRP, N_SHARD, CAP))
    owners = jnp.concatenate([hot_part, others], axis=2).reshape(N_GRP * N_SHARD, LOOK_DEV)
    perm_keys = jax.random.split(jax.random.fold_in(base_key, 3), N_GRP * N_SHARD)
    orders = jax.vmap(lambda perm_key: jax.random.permutation(perm_key, LOOK_DEV))(perm_keys)
    owners = jnp.take_along_axis(owners, orders, axis=1).reshape(N_GRP, N_SHARD, LOOK_DEV)
    picks = jax.random.randint(jax.random.fold_in(base_key, 4), (N_GRP, N_SHARD, LOOK_DEV), 0, TOUCH)
    local_rows = listed[owners, picks]
    return (owners * ROWS_DEV + local_rows).astype(jnp.int32)


def levels(rng, shape, cuts, least, top_value):
    level = 1.0
    for axis_at, parts in cuts:
        draws = jax.random.uniform(jax.random.fold_in(jax.random.fold_in(rng, 6), axis_at), (parts,), jnp.float32, least / len(cuts), top_value / len(cuts))
        level = level * jnp.repeat(jnp.exp(draws), shape[axis_at] // parts).reshape((-1,) + (1,) * (len(shape) - 1 - axis_at))
    return level


def length_profile(amount, total, reach, lean):
    portions = [(1 << 20) // math.isqrt(rank ** lean) + 1 for rank in range(2, amount + 1)]
    spare, counts = total - reach - (amount - 1), [1] * (amount - 1)
    while spare > 0:
        free = [i for i in range(amount - 1) if counts[i] < reach]
        pool, remaining = sum([portions[i] for i in free]), spare
        for i in free:
            addition = min(reach - counts[i], max(1, remaining * portions[i] // pool), spare)
            counts[i] = counts[i] + addition
            spare = spare - addition
    return np.array([reach] + counts)


def uneven(key, count, total, limit, slope):
    if count == 2:
        one = jax.random.randint(key, (), max(1, total - limit), min(limit, total - 1) + 1)
        return jnp.stack([one, total - one])
    tallies = jnp.asarray(length_profile(count, total, limit, slope), jnp.int32)
    couples = (count - 1) // 2
    donor, sink = tallies[1:1 + 2 * couples:2], tallies[2:2 + 2 * couples:2]
    margin = jnp.minimum(donor - 1, limit - sink)
    passed = jax.random.randint(jax.random.fold_in(key, 1), (couples,), 0, 1 << 20) % (margin + 1)
    tallies = tallies.at[1:1 + 2 * couples:2].set(donor - passed).at[2:2 + 2 * couples:2].set(sink + passed)
    return tallies[jax.random.permutation(jax.random.fold_in(key, 2), count)]


def bell_draw(own_key, dims, width, reach, pieces=(), held_as=jnp.bfloat16):
    gain = levels(own_key, dims, pieces, -0.22, 0.18) if pieces else 1.0
    entries = jax.random.normal(own_key, dims, jnp.float32) * width * gain
    return jnp.minimum(jnp.maximum(entries, -reach), reach).astype(held_as)


def setup_inputs(seed: int = 0) -> dict:
    key_of = jax.random.split(jax.random.key(seed), 7)
    return {
        "table": bell_draw(key_of[0], (ROWS, E), 1.0, 6.0, ((0, 8),), jnp.float32),
        "accum": jnp.clip(jnp.exp(math.log(2.0) - 3.6888794 * jax.random.uniform(key_of[1], (ROWS,), jnp.float32) ** levels(key_of[1], (ROWS,), ((0, 8),), -0.2, 0.2)), 0.05, 2.0),
        "pooled_grad": bell_draw(key_of[2], (N_GRP, N_SHARD, B_DEV, E), 1.0, 6.0, ((0, 4), (1, 8))),
        "row_ids": draw_row_ids(jax.random.fold_in(key_of[6], 71), 0),
        "bag_ids": jax.vmap(lambda own: jnp.searchsorted(jnp.cumsum(uneven(own, B_DEV, LOOK_DEV, 2 * POOL, 0)), jnp.arange(LOOK_DEV), side="right"))(jax.random.split(key_of[4], N_GRP * N_SHARD)).reshape((N_GRP, N_SHARD, LOOK_DEV)).astype(jnp.int32),
        "touched": draw_touched(jax.random.fold_in(key_of[6], 71), 0),
    }


def reference(table, accum, pooled_grad, row_ids, bag_ids, touched):
    devices_all = N_GRP * N_SHARD
    grads = pooled_grad.reshape(devices_all, B_DEV, E)
    samples = bag_ids.reshape(devices_all, LOOK_DEV)
    values = jax.vmap(lambda grad_block, sample_ids: jnp.take(grad_block, sample_ids, axis=0))(grads, samples)
    values = values.reshape(-1, E).astype(jnp.float32)
    flat_ids = row_ids.reshape(-1)
    dense = jnp.zeros((ROWS, E), jnp.float32).at[flat_ids].add(values)
    shard_base = (jnp.arange(N_SHARD, dtype=jnp.int32) * ROWS_DEV)[:, None]
    listed_rows = (touched + shard_base).reshape(-1).astype(jnp.int32)
    keep = jnp.zeros((ROWS,), jnp.float32).at[listed_rows].set(1.0)
    grad_rows = dense * keep[:, None]
    new_accum = accum + lax.optimization_barrier(jnp.mean(grad_rows * grad_rows, axis=1))
    new_table = table - 0.5 * grad_rows / (jnp.sqrt(new_accum)[:, None] + 1e-08)
    return (new_table, new_accum)
```

```python
import functools

import jax
import jax.numpy as jnp
from jax import lax
from jax.experimental import pallas as pl
from jax.experimental.pallas import tpu as pltpu
from jax.sharding import PartitionSpec as P

LANES = 128
MESH = pl.DeviceIdType.MESH
NT = (((1,), (1,)), ((), ()))


def log2(n):
    return n.bit_length() - 1


def grid_of(shards):
    x = 1
    while 4 * x * x <= shards:
        x *= 2
    return shards // x, x


def onehot(mask):
    return jnp.where(mask, 1.0, 0.0).astype(jnp.bfloat16)


def iota(shape, dim):
    return lax.broadcasted_iota(jnp.int32, shape, dim)


def route(ids_ref, bags_ref, shards, rows_dev, cap, left, right):
    lines = ids_ref.shape[0]
    ids, bags = ids_ref[...], bags_ref[...]
    owner = ids >> log2(rows_dev)
    local = ids & (rows_dev - 1)
    owned = [onehot(owner == s) for s in range(shards)]
    owned = jnp.concatenate(owned, axis=0)
    total = shards * lines
    before = onehot(iota((LANES, LANES), 0) < iota((LANES, LANES), 1))
    a, b = iota((total, total), 0), iota((total, total), 1)
    above = onehot(((a >> log2(lines)) == (b >> log2(lines))) & (b < a))
    counts = jnp.dot(above, owned, preferred_element_type=jnp.float32)
    offset = jnp.sum(counts, axis=1, keepdims=True)
    rank = jnp.dot(owned, before, preferred_element_type=jnp.float32) + offset
    slot = jnp.zeros((lines, LANES), jnp.float32)
    for s in range(shards):
        part = slice(s * lines, (s + 1) * lines)
        slot = slot + owned[part].astype(jnp.float32) * (rank[part] + float(s * cap))
    slot = slot.astype(jnp.int32)
    groups = shards * cap // LANES
    high, low = slot >> 7, slot & (LANES - 1)
    parts = [
        (local & 127).astype(jnp.float32),
        ((local >> 7) + 1).astype(jnp.float32),
        (bags & 127).astype(jnp.float32),
        (bags >> 7).astype(jnp.float32),
    ]
    group_no = iota((groups, LANES), 0)
    lane_no = iota((LANES, LANES), 0)
    for i in range(lines):
        at = slice(i * LANES, (i + 1) * LANES)
        hit = high[i : i + 1] == group_no
        for p, value in enumerate(parts):
            left[p * groups : (p + 1) * groups, at] = jnp.where(
                hit, value[i : i + 1], 0.0
            ).astype(jnp.bfloat16)
        right[:, at] = onehot(low[i : i + 1] == lane_no)
    placed = lax.dot_general(left[...], right[...], NT, preferred_element_type=jnp.float32)
    rows = (placed[groups : 2 * groups] - 1.0) * 128.0 + placed[:groups]
    samples = placed[3 * groups :] * 128.0 + placed[2 * groups : 3 * groups]
    return rows, samples


def share_kernel(
    shards, n_grp, rows_dev, cap, cut, chunks,
    g_ref, ids_ref, bags_ref, listed_ref, out_ref,
    blocks, tiles_out, tiles_in, left, right, listed_col, bag_hot, count, acc,
    sib_in, y_sums, final, sib_out,
    block_send, block_recv, tile_send, tile_recv, s1, r1, s2, r2, s3, r3,
):
    nz, nx = grid_of(shards)
    ny = n_grp // 2
    me = lax.axis_index("shard")
    grp = lax.axis_index("grp")
    z, x = me // nx, me % nx
    y, core = grp // 2, grp % 2
    samples, width = g_ref.shape
    touch = acc.shape[0]
    half = touch // 2
    piece = half // chunks
    other = (me + 1) % shards
    sibling = y * 2 + (1 - core)

    barrier = pltpu.get_barrier_semaphore()

    def greet_shard(o, c):
        pl.semaphore_signal(barrier, 1, device_id={"shard": (me + o) % shards}, device_id_type=MESH)
        return c

    def greet_grp(o, c):
        pl.semaphore_signal(barrier, 1, device_id={"grp": (grp + o) % n_grp}, device_id_type=MESH)
        return c

    lax.fori_loop(1, shards, greet_shard, 0)
    lax.fori_loop(1, n_grp, greet_grp, 0)
    blocks[me] = g_ref[...]
    pl.semaphore_wait(barrier, shards + n_grp - 2)

    spans = (pl.ds(0, cut), pl.ds(cut, samples - cut))

    def block_copy(part, src, way, to):
        where = blocks.at[src, spans[part]]
        return pltpu.make_async_remote_copy(
            src_ref=where,
            dst_ref=where,
            send_sem=block_send.at[part, src, way],
            recv_sem=block_recv.at[part, src],
            device_id={"shard": to},
            device_id_type=MESH,
        )

    def ways(part, zs, xs):
        on_z = (x == xs) if part == 0 else (z >= 0)
        on_x = (z == zs) if part == 1 else (x >= 0)
        return (
            (on_z & (z >= zs) & (z + 1 < nz), me + nx),
            (on_z & (z <= zs) & (z >= 1), me - nx),
            (on_x & (x >= xs) & (x + 1 < nx), me + 1),
            (on_x & (x <= xs) & (x >= 1), me - 1),
        )

    def forward(part, src, zs, xs):
        for way, (when, to) in enumerate(ways(part, zs, xs)):

            @pl.when(when)
            def _():
                block_copy(part, src, way, to).start()

    for part in (0, 1):
        forward(part, me, z, x)

    rows, bags = route(ids_ref, bags_ref, shards, rows_dev, cap, left, right)
    per = cap // LANES
    for s in range(shards):
        tiles_out[s, :per] = rows[s * per : (s + 1) * per]
        tiles_out[s, per:] = bags[s * per : (s + 1) * per]

    def tile_copy(dst):
        return pltpu.make_async_remote_copy(
            src_ref=tiles_out.at[dst],
            dst_ref=tiles_in.at[me],
            send_sem=tile_send.at[dst],
            recv_sem=tile_recv.at[me],
            device_id={"shard": dst},
            device_id_type=MESH,
        )

    def send_tile(o, c):
        tile_copy((me + o) % shards).start()
        return c

    lax.fori_loop(1, shards, send_tile, 0)
    tiles_in[me] = tiles_out[me]

    listed = listed_ref[...].astype(jnp.float32)
    for j in range(touch // LANES):
        listed_col[j * LANES : (j + 1) * LANES] = jnp.broadcast_to(
            listed[j : j + 1], (LANES, LANES)
        ).T
    acc[...] = jnp.zeros_like(acc)
    bag_no = iota((samples, LANES), 0).astype(jnp.float32)

    def one_source(src, zs, xs, own):
        @pl.when(jnp.logical_not(own))
        def _():
            pltpu.make_async_remote_copy(
                src_ref=tiles_out.at[src],
                dst_ref=tiles_in.at[src],
                send_sem=tile_send.at[src],
                recv_sem=tile_recv.at[src],
                device_id={"shard": other},
                device_id_type=MESH,
            ).wait_recv()

        tile = tiles_in[src]
        for c in range(per):
            bag_hot[:, c * LANES : (c + 1) * LANES] = onehot(bag_no == tile[per + c : per + c + 1])

        def build(k, carry):
            at = pl.ds(pl.multiple_of(k * LANES, LANES), LANES)
            col = listed_col[at]
            hits = [onehot(col == tile[c : c + 1]) for c in range(per)]
            found = lax.dot_general(
                jnp.concatenate(hits, axis=1), bag_hot[...], NT, preferred_element_type=jnp.float32
            )
            count[at] = found.astype(jnp.bfloat16)
            return carry

        lax.fori_loop(0, touch // LANES, build, 0)

        @pl.when(jnp.logical_not(own))
        def _():
            for part in (0, 1):
                block_copy(part, src, 0, other).wait_recv()
                forward(part, src, zs, xs)

        def add(k, carry):
            at = pl.ds(pl.multiple_of(k * LANES, LANES), LANES)
            acc[at] += jnp.dot(count[at], blocks[src], preferred_element_type=jnp.float32)
            return carry

        lax.fori_loop(0, touch // LANES, add, 0)

    def by_distance(i, carry):
        d = i // (2 * nx)
        xo = (i // 2) % nx
        zs = z + d * (1 - 2 * (i % 2))
        xs = (x + xo) % nx
        valid = (zs >= 0) & (zs < nz) & ((d > 0) | (i % 2 == 0))

        @pl.when(valid)
        def _():
            one_source(zs * nx + xs, zs, xs, (d == 0) & (xo == 0))

        return carry

    lax.fori_loop(0, 2 * nx * nz, by_distance, 0)

    def rows_at(base, c):
        return pl.ds(pl.multiple_of(base * half + c * piece, piece), piece)

    def first_copy(c):
        return pltpu.make_async_remote_copy(
            src_ref=acc.at[rows_at(1 - core, c)],
            dst_ref=sib_in.at[rows_at(0, c)],
            send_sem=s1.at[c],
            recv_sem=r1.at[c],
            device_id={"grp": sibling},
            device_id_type=MESH,
        )

    def y_copy(c, to_y, from_y):
        where = y_sums.at[from_y, rows_at(0, c)]
        return pltpu.make_async_remote_copy(
            src_ref=where,
            dst_ref=where,
            send_sem=s2.at[to_y, c],
            recv_sem=r2.at[from_y, c],
            device_id={"grp": to_y * 2 + core},
            device_id_type=MESH,
        )

    def last_copy(c):
        return pltpu.make_async_remote_copy(
            src_ref=final.at[rows_at(0, c)],
            dst_ref=sib_out.at[rows_at(0, c)],
            send_sem=s3.at[c],
            recv_sem=r3.at[c],
            device_id={"grp": sibling},
            device_id_type=MESH,
        )

    for c in range(chunks):
        first_copy(c).start()
    for c in range(chunks):
        first_copy(c).wait_recv()
        y_sums[y, rows_at(0, c)] = acc[rows_at(core, c)] + sib_in[rows_at(0, c)]
        for o in range(1, ny):
            y_copy(c, (y + o) % ny, y).start()
    for c in range(chunks):
        for o in range(1, ny):
            from_y = (y + o) % ny
            y_copy(c, from_y, from_y).wait_recv()
        total = y_sums[0, rows_at(0, c)]
        for k in range(1, ny):
            total = total + y_sums[k, rows_at(0, c)]
        final[rows_at(0, c)] = total
        last_copy(c).start()
        out_ref[rows_at(core, c)] = total
    for c in range(chunks):
        last_copy(c).wait_recv()
        out_ref[rows_at(1 - core, c)] = sib_out[rows_at(0, c)]

    for c in range(chunks):
        first_copy(c).wait_send()
        for o in range(1, ny):
            y_copy(c, (y + o) % ny, y).wait_send()
        last_copy(c).wait_send()

    def tile_sent(o, carry):
        tile_copy((me + o) % shards).wait_send()
        return carry

    lax.fori_loop(1, shards, tile_sent, 0)

    def block_sent(src, carry):
        for part in (0, 1):
            for way, (when, to) in enumerate(ways(part, src // nx, src % nx)):

                @pl.when(when)
                def _():
                    block_copy(part, src, way, to).wait_send()

        return carry

    lax.fori_loop(0, shards, block_sent, 0)


def summed(grads, ids, bags, listed, shards, n_grp, rows_dev):
    samples, width = grads.shape
    looks = ids.size
    touch = listed.size
    cap = looks // 8
    groups = shards * cap // LANES
    half = touch // 2
    chunks = 4
    cut = samples // 2
    f32, bf16 = jnp.float32, jnp.bfloat16
    vmem = pl.BlockSpec(memory_space=pltpu.VMEM)
    dma = pltpu.SemaphoreType.DMA
    return pl.pallas_call(
        functools.partial(share_kernel, shards, n_grp, rows_dev, cap, cut, chunks),
        out_shape=jax.ShapeDtypeStruct((touch, width), f32),
        in_specs=[vmem] * 4,
        out_specs=vmem,
        scratch_shapes=[
            pltpu.VMEM((shards, samples, width), bf16),
            pltpu.VMEM((shards, 2 * cap // LANES, LANES), f32),
            pltpu.VMEM((shards, 2 * cap // LANES, LANES), f32),
            pltpu.VMEM((4 * groups, looks), bf16),
            pltpu.VMEM((LANES, looks), bf16),
            pltpu.VMEM((touch, LANES), f32),
            pltpu.VMEM((samples, cap), bf16),
            pltpu.VMEM((touch, samples), bf16),
            pltpu.VMEM((touch, width), f32),
            pltpu.VMEM((half, width), f32),
            pltpu.VMEM((n_grp // 2, half, width), f32),
            pltpu.VMEM((half, width), f32),
            pltpu.VMEM((half, width), f32),
            dma((2, shards, 4)),
            dma((2, shards)),
            dma((shards,)),
            dma((shards,)),
            dma((chunks,)),
            dma((chunks,)),
            dma((n_grp // 2, chunks)),
            dma((n_grp // 2, chunks)),
            dma((chunks,)),
            dma((chunks,)),
        ],
        compiler_params=pltpu.CompilerParams(
            collective_id=0, has_side_effects=True, vmem_limit_bytes=48 * 2**20
        ),
    )(grads, ids, bags, listed)


def update_kernel(first_ref, table_ref, accum_ref, sums_ref, listed_ref, new_ref, new_accum_ref, halves):
    step = pl.program_id(0)
    width = table_ref.shape[1]
    blocks = table_ref.shape[0] // LANES

    @pl.when(step == 0)
    def _():
        sums = sums_ref[...]
        high = sums.astype(jnp.bfloat16)
        halves[:, :width] = high
        halves[:, width:] = (sums - high.astype(jnp.float32)).astype(jnp.bfloat16)

    for b in range(blocks):
        at = slice(b * LANES, (b + 1) * LANES)
        block = step * blocks + b
        first = first_ref[block]
        row_no = iota((LANES, LANES), 0) + block * LANES
        hot = [onehot(listed_ref[pl.ds(first + w, 1)] == row_no) for w in range(2)]
        found = jnp.dot(
            jnp.concatenate(hot, axis=1),
            halves[pl.ds(pl.multiple_of(first * LANES, LANES), 2 * LANES)],
            preferred_element_type=jnp.float32,
        )
        grads = found[:, :width] + found[:, width:]
        mean = jnp.sum(grads * grads, axis=1, keepdims=True) * (1.0 / width)
        accum = jnp.broadcast_to(accum_ref[b : b + 1], (LANES, LANES)).T
        accum_next = accum + mean
        scale = 0.5 / (jnp.sqrt(accum_next) + 1e-08)
        for w in range(width // LANES):
            cols = slice(w * LANES, (w + 1) * LANES)
            new_ref[at, cols] = table_ref[at, cols] - grads[:, cols] * scale
        new_accum_ref[b : b + 1] = accum_next.T[:1]


def update(table, accum, sums, listed, first):
    rows, width = table.shape
    touch = sums.shape[0]
    block = 1024
    lines = block // LANES
    return pl.pallas_call(
        update_kernel,
        grid_spec=pltpu.PrefetchScalarGridSpec(
            num_scalar_prefetch=1,
            grid=(rows // block,),
            in_specs=[
                pl.BlockSpec((block, width), lambda i, s: (i, 0)),
                pl.BlockSpec((lines, LANES), lambda i, s: (i, 0)),
                pl.BlockSpec((touch, width), lambda i, s: (0, 0)),
                pl.BlockSpec((touch // LANES, LANES), lambda i, s: (0, 0)),
            ],
            out_specs=[
                pl.BlockSpec((block, width), lambda i, s: (i, 0)),
                pl.BlockSpec((lines, LANES), lambda i, s: (i, 0)),
            ],
            scratch_shapes=[pltpu.VMEM((touch, 2 * width), jnp.bfloat16)],
        ),
        out_shape=[
            jax.ShapeDtypeStruct((rows, width), jnp.float32),
            jax.ShapeDtypeStruct((rows // LANES, LANES), jnp.float32),
        ],
        compiler_params=pltpu.CompilerParams(vmem_limit_bytes=32 * 2**20),
    )(first, table, accum, sums, listed)


def body(shards, n_grp, table, accum, pooled_grad, row_ids, bag_ids, touched):
    rows_dev, width = table.shape
    grads = pooled_grad.reshape(-1, width)
    ids = row_ids.reshape(-1, LANES)
    bags = bag_ids.reshape(-1, LANES)
    listed = touched.reshape(-1, LANES)
    sums = summed(grads, ids, bags, listed, shards, n_grp, rows_dev)
    starts = jnp.arange(rows_dev // LANES, dtype=jnp.int32) * LANES
    below = jnp.sum((touched.reshape(1, -1) < starts[:, None]).astype(jnp.int32), axis=1)
    first = jnp.minimum(below // LANES, listed.shape[0] - 2)
    new_table, new_accum = update(table, accum.reshape(-1, LANES), sums, listed, first)
    return new_table, new_accum.reshape(-1)


def solution(mesh):
    return jax.shard_map(
        functools.partial(body, mesh.shape["shard"], mesh.shape["grp"]),
        mesh=mesh,
        in_specs=(
            P("shard", None),
            P("shard"),
            P("grp", "shard", None, None),
            P("grp", "shard", None),
            P("grp", "shard", None),
            P("shard", None),
        ),
        out_specs=(P("shard", None), P("shard")),
        check_vma=False,
    )
```

```python
import functools

import jax
import jax.numpy as jnp
from jax import lax
from jax.experimental import pallas as pl
from jax.experimental.pallas import tpu as pltpu
from jax.sharding import PartitionSpec as P

LANES = 128
MESH = pl.DeviceIdType.MESH
NT = (((1,), (1,)), ((), ()))


def log2(n):
    return n.bit_length() - 1


def grid_of(shards):
    x = 1
    while 4 * x * x <= shards:
        x *= 2
    return shards // x, x


def onehot(mask):
    return jnp.where(mask, 1.0, 0.0).astype(jnp.bfloat16)


def iota(shape, dim):
    return lax.broadcasted_iota(jnp.int32, shape, dim)


def route(ids_ref, bags_ref, shards, rows_dev, cap, left, right):
    lines = ids_ref.shape[0]
    ids, bags = ids_ref[...], bags_ref[...]
    owner = ids >> log2(rows_dev)
    local = ids & (rows_dev - 1)
    owned = [onehot(owner == s) for s in range(shards)]
    owned = jnp.concatenate(owned, axis=0)
    total = shards * lines
    before = onehot(iota((LANES, LANES), 0) < iota((LANES, LANES), 1))
    a, b = iota((total, total), 0), iota((total, total), 1)
    above = onehot(((a >> log2(lines)) == (b >> log2(lines))) & (b < a))
    counts = jnp.dot(above, owned, preferred_element_type=jnp.float32)
    offset = jnp.sum(counts, axis=1, keepdims=True)
    rank = jnp.dot(owned, before, preferred_element_type=jnp.float32) + offset
    slot = jnp.zeros((lines, LANES), jnp.float32)
    for s in range(shards):
        part = slice(s * lines, (s + 1) * lines)
        slot = slot + owned[part].astype(jnp.float32) * (rank[part] + float(s * cap))
    slot = slot.astype(jnp.int32)
    groups = shards * cap // LANES
    high, low = slot >> 7, slot & (LANES - 1)
    parts = [
        (local & 127).astype(jnp.float32),
        ((local >> 7) + 1).astype(jnp.float32),
        (bags & 127).astype(jnp.float32),
        (bags >> 7).astype(jnp.float32),
    ]
    group_no = iota((groups, LANES), 0)
    lane_no = iota((LANES, LANES), 0)
    for i in range(lines):
        at = slice(i * LANES, (i + 1) * LANES)
        hit = high[i : i + 1] == group_no
        for p, value in enumerate(parts):
            left[p * groups : (p + 1) * groups, at] = jnp.where(
                hit, value[i : i + 1], 0.0
            ).astype(jnp.bfloat16)
        right[:, at] = onehot(low[i : i + 1] == lane_no)
    placed = lax.dot_general(left[...], right[...], NT, preferred_element_type=jnp.float32)
    rows = (placed[groups : 2 * groups] - 1.0) * 128.0 + placed[:groups]
    samples = placed[3 * groups :] * 128.0 + placed[2 * groups : 3 * groups]
    return rows, samples


def share_kernel(
    shards, n_grp, rows_dev, cap, cuts, chunks,
    g_hbm, ids_hbm, bags_hbm, listed_hbm, out_ref,
    ids_ref, bags_ref, listed_ref,
    blocks, tiles_out, tiles_in, left, right, listed_col, bag_hot, row_hot, picked, acc,
    sib_in, y_sums, final, sib_out,
    load_sem, block_send, block_recv, tile_send, tile_recv, s1, r1, s2, r2, s3, r3,
):
    nz, nx = grid_of(shards)
    ny = n_grp // 2
    me = lax.axis_index("shard")
    grp = lax.axis_index("grp")
    z, x = me // nx, me % nx
    y, core = grp // 2, grp % 2
    samples, width = g_hbm.shape
    touch = acc.shape[0]
    half = touch // 2
    piece = half // chunks
    other = (me + 1) % shards
    sibling = y * 2 + (1 - core)

    loads = [
        pltpu.make_async_copy(src, dst, load_sem.at[i])
        for i, (src, dst) in enumerate(
            [
                (g_hbm, blocks.at[me]),
                (ids_hbm, ids_ref),
                (bags_hbm, bags_ref),
                (listed_hbm, listed_ref),
            ]
        )
    ]
    for load in loads:
        load.start()

    barrier = pltpu.get_barrier_semaphore()

    def greet_shard(o, c):
        pl.semaphore_signal(barrier, 1, device_id={"shard": (me + o) % shards}, device_id_type=MESH)
        return c

    def greet_grp(o, c):
        pl.semaphore_signal(barrier, 1, device_id={"grp": (grp + o) % n_grp}, device_id_type=MESH)
        return c

    lax.fori_loop(1, shards, greet_shard, 0)
    lax.fori_loop(1, n_grp, greet_grp, 0)
    pl.semaphore_wait(barrier, shards + n_grp - 2)
    loads[0].wait()

    edges = (0, *cuts, samples)
    spans = [pl.ds(a, b - a) for a, b in zip(edges, edges[1:])]
    parts = range(len(spans))

    def block_copy(part, src, way, to):
        where = blocks.at[src, spans[part]]
        return pltpu.make_async_remote_copy(
            src_ref=where,
            dst_ref=where,
            send_sem=block_send.at[part, src, way],
            recv_sem=block_recv.at[part, src],
            device_id={"shard": to},
            device_id_type=MESH,
        )

    def ways(part, zs, xs):
        on_z = (x == xs) if part % 2 == 0 else (z >= 0)
        on_x = (z == zs) if part % 2 == 1 else (x >= 0)
        return (
            (on_z & (z >= zs) & (z + 1 < nz), me + nx),
            (on_z & (z <= zs) & (z >= 1), me - nx),
            (on_x & (x >= xs) & (x + 1 < nx), me + 1),
            (on_x & (x <= xs) & (x >= 1), me - 1),
        )

    def forward(part, src, zs, xs):
        for way, (when, to) in enumerate(ways(part, zs, xs)):

            @pl.when(when)
            def _():
                block_copy(part, src, way, to).start()

    for part in parts:
        forward(part, me, z, x)

    for load in loads[1:]:
        load.wait()
    rows, bags = route(ids_ref, bags_ref, shards, rows_dev, cap, left, right)
    per = cap // LANES
    for s in range(shards):
        tiles_out[s, :per] = rows[s * per : (s + 1) * per]
        tiles_out[s, per:] = bags[s * per : (s + 1) * per]

    def tile_copy(dst):
        return pltpu.make_async_remote_copy(
            src_ref=tiles_out.at[dst],
            dst_ref=tiles_in.at[me],
            send_sem=tile_send.at[dst],
            recv_sem=tile_recv.at[me],
            device_id={"shard": dst},
            device_id_type=MESH,
        )

    def send_tile(o, c):
        tile_copy((me + o) % shards).start()
        return c

    lax.fori_loop(1, shards, send_tile, 0)
    tiles_in[me] = tiles_out[me]

    listed = listed_ref[...].astype(jnp.float32)
    for j in range(touch // LANES):
        listed_col[j * LANES : (j + 1) * LANES] = jnp.broadcast_to(
            listed[j : j + 1], (LANES, LANES)
        ).T
    acc[...] = jnp.zeros_like(acc)
    bag_no = iota((LANES, samples), 1).astype(jnp.float32)
    half_rows = touch // 2

    def one_source(src, zs, xs, own):
        @pl.when(jnp.logical_not(own))
        def _():
            pltpu.make_async_remote_copy(
                src_ref=tiles_out.at[src],
                dst_ref=tiles_in.at[src],
                send_sem=tile_send.at[src],
                recv_sem=tile_recv.at[src],
                device_id={"shard": other},
                device_id_type=MESH,
            ).wait_recv()

        tile = tiles_in[src]
        for c in range(per):
            column = jnp.broadcast_to(tile[per + c : per + c + 1], (LANES, LANES)).T
            bag_hot[c * LANES : (c + 1) * LANES] = onehot(bag_no == column[:, :1])

        def build(k, carry):
            at = pl.ds(pl.multiple_of(k * LANES, LANES), LANES)
            col = listed_col[at]
            for c in range(per):
                row_hot[at, c * LANES : (c + 1) * LANES] = onehot(col == tile[c : c + 1])
            return carry

        lax.fori_loop(0, touch // LANES, build, 0)

        @pl.when(jnp.logical_not(own))
        def _():
            for part in parts:
                block_copy(part, src, 0, other).wait_recv()
                forward(part, src, zs, xs)

        picked[...] = jnp.dot(
            bag_hot[...], blocks[src], preferred_element_type=jnp.float32
        ).astype(jnp.bfloat16)
        for h in range(2):
            at = slice(h * half_rows, (h + 1) * half_rows)
            acc[at] += jnp.dot(row_hot[at], picked[...], preferred_element_type=jnp.float32)

    def by_distance(i, carry):
        d = i // (2 * nx)
        xo = (i // 2) % nx
        zs = z + d * (1 - 2 * (i % 2))
        xs = (x + xo) % nx
        valid = (zs >= 0) & (zs < nz) & ((d > 0) | (i % 2 == 0))

        @pl.when(valid)
        def _():
            one_source(zs * nx + xs, zs, xs, (d == 0) & (xo == 0))

        return carry

    lax.fori_loop(0, 2 * nx * nz, by_distance, 0)

    def rows_at(base, c):
        return pl.ds(pl.multiple_of(base * half + c * piece, piece), piece)

    def first_copy(c):
        return pltpu.make_async_remote_copy(
            src_ref=acc.at[rows_at(1 - core, c)],
            dst_ref=sib_in.at[rows_at(0, c)],
            send_sem=s1.at[c],
            recv_sem=r1.at[c],
            device_id={"grp": sibling},
            device_id_type=MESH,
        )

    def y_copy(c, to_y, from_y):
        where = y_sums.at[from_y, rows_at(0, c)]
        return pltpu.make_async_remote_copy(
            src_ref=where,
            dst_ref=where,
            send_sem=s2.at[to_y, c],
            recv_sem=r2.at[from_y, c],
            device_id={"grp": to_y * 2 + core},
            device_id_type=MESH,
        )

    def last_copy(c):
        return pltpu.make_async_remote_copy(
            src_ref=final.at[rows_at(0, c)],
            dst_ref=sib_out.at[rows_at(0, c)],
            send_sem=s3.at[c],
            recv_sem=r3.at[c],
            device_id={"grp": sibling},
            device_id_type=MESH,
        )

    for c in range(chunks):
        first_copy(c).start()
    for c in range(chunks):
        first_copy(c).wait_recv()
        y_sums[y, rows_at(0, c)] = acc[rows_at(core, c)] + sib_in[rows_at(0, c)]
        for o in range(1, ny):
            y_copy(c, (y + o) % ny, y).start()
    for c in range(chunks):
        for o in range(1, ny):
            from_y = (y + o) % ny
            y_copy(c, from_y, from_y).wait_recv()
        total = y_sums[0, rows_at(0, c)]
        for k in range(1, ny):
            total = total + y_sums[k, rows_at(0, c)]
        final[rows_at(0, c)] = total
        last_copy(c).start()
        out_ref[rows_at(core, c)] = total
    for c in range(chunks):
        last_copy(c).wait_recv()
        out_ref[rows_at(1 - core, c)] = sib_out[rows_at(0, c)]

    for c in range(chunks):
        first_copy(c).wait_send()
        for o in range(1, ny):
            y_copy(c, (y + o) % ny, y).wait_send()
        last_copy(c).wait_send()

    def tile_sent(o, carry):
        tile_copy((me + o) % shards).wait_send()
        return carry

    lax.fori_loop(1, shards, tile_sent, 0)

    def block_sent(src, carry):
        for part in parts:
            for way, (when, to) in enumerate(ways(part, src // nx, src % nx)):

                @pl.when(when)
                def _():
                    block_copy(part, src, way, to).wait_send()

        return carry

    lax.fori_loop(0, shards, block_sent, 0)


def summed(grads, ids, bags, listed, shards, n_grp, rows_dev):
    samples, width = grads.shape
    looks = ids.size
    touch = listed.size
    cap = looks // 8
    groups = shards * cap // LANES
    half = touch // 2
    chunks = 4
    cuts = (samples * 5 // 16, samples // 2, samples * 25 // 32)
    f32, bf16 = jnp.float32, jnp.bfloat16
    vmem = pl.BlockSpec(memory_space=pltpu.VMEM)
    dma = pltpu.SemaphoreType.DMA
    return pl.pallas_call(
        functools.partial(share_kernel, shards, n_grp, rows_dev, cap, cuts, chunks),
        out_shape=jax.ShapeDtypeStruct((touch, width), f32),
        in_specs=[pl.BlockSpec(memory_space=pl.ANY)] * 4,
        out_specs=vmem,
        scratch_shapes=[
            pltpu.VMEM(ids.shape, jnp.int32),
            pltpu.VMEM(bags.shape, jnp.int32),
            pltpu.VMEM(listed.shape, jnp.int32),
            pltpu.VMEM((shards, samples, width), bf16),
            pltpu.VMEM((shards, 2 * cap // LANES, LANES), f32),
            pltpu.VMEM((shards, 2 * cap // LANES, LANES), f32),
            pltpu.VMEM((4 * groups, looks), bf16),
            pltpu.VMEM((LANES, looks), bf16),
            pltpu.VMEM((touch, LANES), f32),
            pltpu.VMEM((cap, samples), bf16),
            pltpu.VMEM((touch, cap), bf16),
            pltpu.VMEM((cap, width), bf16),
            pltpu.VMEM((touch, width), f32),
            pltpu.VMEM((half, width), f32),
            pltpu.VMEM((n_grp // 2, half, width), f32),
            pltpu.VMEM((half, width), f32),
            pltpu.VMEM((half, width), f32),
            dma((4,)),
            dma((len(cuts) + 1, shards, 4)),
            dma((len(cuts) + 1, shards)),
            dma((shards,)),
            dma((shards,)),
            dma((chunks,)),
            dma((chunks,)),
            dma((n_grp // 2, chunks)),
            dma((n_grp // 2, chunks)),
            dma((chunks,)),
            dma((chunks,)),
        ],
        compiler_params=pltpu.CompilerParams(
            collective_id=0, has_side_effects=True, vmem_limit_bytes=60 * 2**20
        ),
    )(grads, ids, bags, listed)


def update_kernel(table_ref, accum_ref, sums_ref, listed_ref, new_ref, new_accum_ref, halves):
    step = pl.program_id(0)
    width = table_ref.shape[1]
    blocks = table_ref.shape[0] // LANES

    @pl.when(step == 0)
    def _():
        sums = sums_ref[...]
        high = sums.astype(jnp.bfloat16)
        halves[:, :width] = high
        halves[:, width:] = (sums - high.astype(jnp.float32)).astype(jnp.bfloat16)

    for b in range(blocks):
        at = slice(b * LANES, (b + 1) * LANES)
        block = step * blocks + b
        below = jnp.sum(jnp.where(listed_ref[...] < block * LANES, 1.0, 0.0)).astype(jnp.int32)
        first = jnp.minimum(below >> 7, listed_ref.shape[0] - 2)
        row_no = iota((LANES, LANES), 0) + block * LANES
        hot = [onehot(listed_ref[pl.ds(first + w, 1)] == row_no) for w in range(2)]
        found = jnp.dot(
            jnp.concatenate(hot, axis=1),
            halves[pl.ds(pl.multiple_of(first * LANES, LANES), 2 * LANES)],
            preferred_element_type=jnp.float32,
        )
        grads = found[:, :width] + found[:, width:]
        mean = jnp.sum(grads * grads, axis=1, keepdims=True) * (1.0 / width)
        accum = jnp.broadcast_to(accum_ref[b : b + 1], (LANES, LANES)).T
        accum_next = accum + mean
        scale = 0.5 / (jnp.sqrt(accum_next) + 1e-08)
        for w in range(width // LANES):
            cols = slice(w * LANES, (w + 1) * LANES)
            new_ref[at, cols] = table_ref[at, cols] - grads[:, cols] * scale
        new_accum_ref[b : b + 1] = accum_next.T[:1]


def update(table, accum, sums, listed):
    rows, width = table.shape
    touch = sums.shape[0]
    block = 1024
    lines = block // LANES
    return pl.pallas_call(
        update_kernel,
        grid_spec=pl.GridSpec(
            grid=(rows // block,),
            in_specs=[
                pl.BlockSpec((block, width), lambda i: (i, 0)),
                pl.BlockSpec((lines, LANES), lambda i: (i, 0)),
                pl.BlockSpec((touch, width), lambda i: (0, 0)),
                pl.BlockSpec((touch // LANES, LANES), lambda i: (0, 0)),
            ],
            out_specs=[
                pl.BlockSpec((block, width), lambda i: (i, 0)),
                pl.BlockSpec((lines, LANES), lambda i: (i, 0)),
            ],
            scratch_shapes=[pltpu.VMEM((touch, 2 * width), jnp.bfloat16)],
        ),
        out_shape=[
            jax.ShapeDtypeStruct((rows, width), jnp.float32),
            jax.ShapeDtypeStruct((rows // LANES, LANES), jnp.float32),
        ],
        compiler_params=pltpu.CompilerParams(vmem_limit_bytes=60 * 2**20),
    )(table, accum, sums, listed)


def body(shards, n_grp, table, accum, pooled_grad, row_ids, bag_ids, touched):
    rows_dev, width = table.shape
    grads = pooled_grad.reshape(-1, width)
    ids = row_ids.reshape(-1, LANES)
    bags = bag_ids.reshape(-1, LANES)
    listed = touched.reshape(-1, LANES)
    sums = summed(grads, ids, bags, listed, shards, n_grp, rows_dev)
    new_table, new_accum = update(table, accum.reshape(-1, LANES), sums, listed)
    return new_table, new_accum.reshape(-1)


def solution(mesh):
    return jax.shard_map(
        functools.partial(body, mesh.shape["shard"], mesh.shape["grp"]),
        mesh=mesh,
        in_specs=(
            P("shard", None),
            P("shard"),
            P("grp", "shard", None, None),
            P("grp", "shard", None),
            P("grp", "shard", None),
            P("shard", None),
        ),
        out_specs=(P("shard", None), P("shard")),
        check_vma=False,
    )
```
